32 devices in a mesh: grp: 2 (over x), row: 16 (over z, y, core).
Axes of the slice: x: 2, y: 2, z: 4, core: 2. Of those that a mesh axis runs over, the one named last changes fastest.
Arguments:
- alignment: bfloat16 [128, 128, 256], P(('grp', 'row')), parts along dimension 0, may hold values from -6 to 6
- seq_flags: int32 [128], P(('grp', 'row')), parts along dimension 0, may hold values 0 or 1
- crop_flags: int32 [256], P('grp'), parts along dimension 0, may hold values 0 or 1
- norm_gain: float32 [256], replicated, may hold values from 0.5 to 1.5
- norm_bias: float32 [256], replicated, may hold values from -3 to 3
- left_weight: bfloat16 [256, 32], replicated, may hold values from -0.375 to 0.375
- left_bias: float32 [32], replicated, may hold values from -3 to 3
- right_weight: bfloat16 [256, 32], replicated, may hold values from -0.375 to 0.375
- right_bias: float32 [32], replicated, may hold values from -3 to 3
- out_weight: bfloat16 [1024, 128], replicated, may hold values from -0.1875 to 0.1875
- out_bias: float32 [128], replicated, may hold values from -3 to 3
Outputs:
- pair_update: bfloat16 [256, 128, 128], P(('grp', 'row')), parts along dimension 0
The draws below stay inside these ranges and needn't reach their ends.
There are 2 independent parts, one for each index of `grp`. The reference program is written for one: setup_inputs(seed, part) draws one part's arguments, and reference() takes and returns one part's arrays. A program takes and returns all parts, laid end to end along the dimension named above; an argument that names none is the same for every part. Nothing has to cross between parts.
All inputs are finite; a program needn't handle non-finite values. No bound on the sum of `seq_flags` on one device may be relied on, other than what follows from the above.
Results may differ from the reference program's by a relative error of at most 0.004.
Values may be sent and summed in bfloat16 or wider, within the bound.
A program may use at most 128 MiB of HBM per device.

```python
import jax
import jax.numpy as jnp
from jax import lax

C_M = 256
C = 32
P_SIZE = 128
RES_DEV = 8
S = 64
R = 128


def touch_ends(drawn, own_key, smallest, largest):
    index_at = [jax.random.randint(jax.random.fold_in(own_key, axis), (), 0, length) for axis, length in enumerate(drawn.shape)]
    main_axis = drawn.shape.index(max(drawn.shape))
    neighbour = index_at[:main_axis] + [(index_at[main_axis] + 1) % drawn.shape[main_axis]] + index_at[main_axis + 1:]
    return drawn.at[tuple(index_at)].set(smallest).at[tuple(neighbour)].set(largest)


def steps_of(rng, dims, split, smallest, high):
    gain, own = 1.0, jax.random.fold_in(rng, 6)
    for position, shards_of in split:
        draws = jnp.exp(jax.random.uniform(jax.random.fold_in(own, position), (shards_of,), jnp.float32, smallest / len(split), high / len(split)))
        gain = gain * jnp.repeat(draws, dims[position] // shards_of).reshape([-1 if axis == position else 1 for axis in range(len(dims))])
    return gain


def centred(own_key, dims, width, most, pieces=(), kind=jnp.bfloat16):
    values = jax.random.normal(own_key, dims, jnp.float32) * width
    if len(pieces) > 0:
        values = steps_of(own_key, dims, pieces, -0.22, 0.18) * values
    return jnp.clip(values, min=-most, max=most).astype(kind)


def setup_inputs(seed: int = 0, part: int = 0) -> dict:
    splits = jax.random.split(jax.random.key(seed), 12)
    part_splits = jax.random.split(jax.random.fold_in(splits[11], part), 12)
    alignment = centred(part_splits[0], (S, R, C_M), 1.0, 6.0, ((0, 16),))
    seq_flags = touch_ends((jax.random.randint(part_splits[1], (S,), 0, 4) < 3).astype(jnp.int32), jax.random.fold_in(part_splits[1], 1), 0, 1)
    crop_flags = touch_ends((jax.random.randint(part_splits[2], (R,), 0, 8) < 7).astype(jnp.int32), jax.random.fold_in(part_splits[2], 1), 0, 1)
    norm_gain = jnp.clip(1.0 + 0.1 * jax.random.normal(splits[3], (C_M,), jnp.float32), 0.5, 1.5)
    norm_bias = centred(splits[4], (C_M,), 0.5, 3.0, (), jnp.float32)
    left_weight = centred(splits[5], (C_M, C), C_M ** -0.5, 0.375)
    left_bias = centred(splits[6], (C,), 0.5, 3.0, (), jnp.float32)
    right_weight = centred(splits[7], (C_M, C), C_M ** -0.5, 0.375)
    right_bias = centred(splits[8], (C,), 0.5, 3.0, (), jnp.float32)
    out_weight = centred(splits[9], (C * C, P_SIZE), (C * C) ** -0.5, 0.1875)
    out_bias = centred(splits[10], (P_SIZE,), 0.5, 3.0, (), jnp.float32)
    return dict(alignment=alignment, seq_flags=seq_flags, crop_flags=crop_flags, norm_gain=norm_gain, norm_bias=norm_bias, left_weight=left_weight, left_bias=left_bias, right_weight=right_weight, right_bias=right_bias, out_weight=out_weight, out_bias=out_bias)


def normalize(values, norm_gain, norm_bias):
    values = values.astype(jnp.float32)
    average = lax.optimization_barrier(jnp.mean(values, axis=-1, keepdims=True))
    variance = lax.optimization_barrier(jnp.mean((values - average) ** 2, axis=-1, keepdims=True))
    return (values - average) * lax.rsqrt(variance + 1e-05) * norm_gain + norm_bias

def project(normed, weight, bias, scaling):
    product = jnp.einsum('src,cd->srd', normed, weight.astype(jnp.float32), precision=lax.Precision.HIGHEST)
    return ((product + bias) * scaling).astype(jnp.bfloat16)

def reference(alignment, seq_flags, crop_flags, norm_gain, norm_bias, left_weight, left_bias, right_weight, right_bias, out_weight, out_bias):
    normed = normalize(alignment, norm_gain, norm_bias)
    crop_float = crop_flags.astype(jnp.float32)
    scaling = seq_flags.astype(jnp.float32)[:, None, None] * crop_float[None, :, None]
    left = project(normed, left_weight, left_bias, scaling)
    right = project(normed, right_weight, right_bias, scaling)
    live_count = jnp.sum(seq_flags.astype(jnp.float32))
    right_flat = right.reshape(S, R * C)

    def row_block(block_index):
        offset = (block_index * RES_DEV).astype(jnp.int32)
        left_block = lax.dynamic_slice_in_dim(left, offset, RES_DEV, 1).reshape(S, RES_DEV * C)
        sums = lax.dot_general(left_block, right_flat, (((0,), (0,)), ((), ())), preferred_element_type=jnp.float32)
        outer_sum = sums.reshape(RES_DEV, C, R, C).transpose(0, 2, 1, 3).reshape(RES_DEV * R, C * C).astype(jnp.bfloat16)
        projected = jnp.dot(outer_sum, out_weight, preferred_element_type=jnp.float32).reshape(RES_DEV, R, P_SIZE)
        crop_rows = lax.dynamic_slice_in_dim(crop_float, offset, RES_DEV, 0)
        divisor = jnp.maximum(live_count * crop_rows[:, None] * crop_float[None, :], 1.0)
        return (projected / divisor[:, :, None] + out_bias).astype(jnp.bfloat16)
    blocks = lax.map(row_block, jnp.arange(R // RES_DEV, dtype=jnp.int32))
    return blocks.reshape(R, R, P_SIZE)
```

```python
import functools

import jax
import jax.numpy as jnp
from jax import lax
from jax.experimental import pallas as pl
from jax.experimental.pallas import tpu as pltpu
from jax.sharding import PartitionSpec as P

LANES = 128
TILE = 16


def copy_plan(steps):
    plan = []
    for a in range(1, steps):
        plan.append(("left", a))
        plan.append(("main", a))
    for a in range(steps):
        plan.append(("side", a))
    for b in range(2):
        for a in range(steps):
            plan.append(("twin", a, b))
    return {name: number for number, name in enumerate(plan)}


def kernel(
    steps,
    flags_ref,
    crop_smem,
    x_ref,
    crop_ref,
    gain_ref,
    shift_ref,
    lw_ref,
    lb_ref,
    rw_ref,
    rb_ref,
    ow_ref,
    ob_ref,
    out_ref,
    held,
    left_src,
    right_f32,
    left_f32,
    weight_f32,
    weight_t,
    outer,
    send_sem,
    recv_sem,
    recv_left,
):
    seqs, residues, width = x_ref.shape
    channels = lw_ref.shape[0]
    rows_here = out_ref.shape[0]
    pair = out_ref.shape[2]
    count = steps * 4
    blocks = residues // LANES
    left_rows = 4 * rows_here
    head = left_rows + TILE
    block_rows = seqs * channels
    total_rows = held.shape[3]
    plan = copy_plan(steps)

    me = lax.axis_index("row")
    core = lax.rem(me, 2)
    side = lax.rem(lax.div(me, 2), 2)
    line = lax.div(me, 4)

    def at_line(offset):
        return lax.rem(line + offset, steps) * 4 + side * 2 + core

    twin = me + 1 - 2 * core
    across = me + 2 - 4 * side

    barrier = pltpu.get_barrier_semaphore()
    peers = [at_line(a) for a in range(1, steps)] + [across, twin]
    for peer in peers:
        pl.semaphore_signal(
            barrier, inc=1, device_id={"row": peer}, device_id_type=pl.DeviceIdType.MESH
        )

    def copy(src, dst, name, recv, device):
        return pltpu.make_async_remote_copy(
            src_ref=src,
            dst_ref=dst,
            send_sem=send_sem.at[plan[name]],
            recv_sem=recv,
            device_id={"row": device},
            device_id_type=pl.DeviceIdType.MESH,
        )

    values = x_ref[...].astype(jnp.float32).reshape(seqs * residues, width)
    average = jnp.mean(values, axis=-1, keepdims=True)
    centred = values - average
    variance = jnp.mean(centred * centred, axis=-1, keepdims=True)
    normed = centred * lax.rsqrt(variance + 1e-05) * gain_ref[...] + shift_ref[...]
    high = normed.astype(jnp.bfloat16)
    low = (normed - high.astype(jnp.float32)).astype(jnp.bfloat16)

    def dot_t(a, b):
        return lax.dot_general(a, b, (((1,), (1,)), ((), ())), preferred_element_type=jnp.float32)

    right = dot_t(rw_ref[...], high) + dot_t(rw_ref[...], low)
    row_of = lax.broadcasted_iota(jnp.int32, (channels, channels), 0)
    col_of = lax.broadcasted_iota(jnp.int32, (channels, channels), 1)
    right_bias = jnp.sum(jnp.where(row_of == col_of, rb_ref[...], 0.0), axis=1, keepdims=True)
    right = right + right_bias
    lane_of = lax.broadcasted_iota(jnp.int32, (TILE, LANES), 1)
    row_id = lax.broadcasted_iota(jnp.int32, (TILE, LANES), 0)
    flag_tile = jnp.zeros((TILE, LANES), jnp.float32)
    for s in range(seqs):
        flag = flags_ref[s].astype(jnp.float32)
        flag_tile = jnp.where((lane_of == s % LANES) & (row_id == s // LANES), flag, flag_tile)
        for b in range(blocks):
            start = s * residues + b * LANES
            piece = (right[:, start : start + LANES] * flag).astype(jnp.bfloat16)
            place = head + b * block_rows + s * channels
            held[0, 0, 0, place : place + channels, :] = piece
    held[0, 0, 0, left_rows:head, :] = flag_tile.astype(jnp.bfloat16)

    left = dot_t(high, lw_ref[...]) + dot_t(low, lw_ref[...]) + lb_ref[...]
    left = jnp.concatenate(
        [left[s * residues : (s + 1) * residues, :] for s in range(seqs)], axis=1
    )
    left_src[...] = left.astype(jnp.bfloat16)
    own = pl.multiple_of(line * left_rows, left_rows)
    held[0, 0, 0, 0:left_rows, :] = left_src[pl.ds(own, left_rows), :]

    pl.semaphore_wait(barrier, len(peers))

    main = pl.ds(left_rows, total_rows - left_rows)
    upper = pl.ds(0, left_rows)
    started = []

    def left_copy(a):
        there = lax.rem(line + a, steps)
        rows = pl.ds(pl.multiple_of(there * left_rows, left_rows), left_rows)
        slot = (steps - a) % steps
        return copy(
            left_src.at[rows, :],
            held.at[slot, 0, 0, upper, :],
            ("left", a),
            recv_left.at[slot],
            at_line(a),
        )

    def main_copy(a):
        slot = (steps - a) % steps
        return copy(
            held.at[0, 0, 0, main, :],
            held.at[slot, 0, 0, main, :],
            ("main", a),
            recv_sem.at[slot, 0, 0],
            at_line(a),
        )

    def side_copy(a):
        return copy(
            held.at[a, 0, 0], held.at[a, 1, 0], ("side", a), recv_sem.at[a, 1, 0], across
        )

    def twin_copy(a, b):
        return copy(
            held.at[a, b, 0], held.at[a, b, 1], ("twin", a, b), recv_sem.at[a, b, 1], twin
        )

    def launch(one):
        one.start()
        started.append(one)

    def absorb(a, b, c):
        k = (c * 2 + b) * steps + a
        for j in range(blocks):
            rows = held[a, b, c, head + j * block_rows : head + (j + 1) * block_rows, :]
            base = (j * count + k) * block_rows
            right_f32[base : base + block_rows, :] = rows.astype(jnp.float32)
        start = pl.multiple_of(side * 2 * rows_here, 2 * rows_here)
        mine = held[a, b, c, pl.ds(start, 2 * rows_here), :].astype(jnp.float32)
        mine = jnp.where(core == 0, mine[:rows_here, :], mine[rows_here:, :])
        left_f32[k * rows_here : (k + 1) * rows_here, :] = mine
        return held[a, b, c, left_rows:head, :].astype(jnp.float32)

    launch(side_copy(0))
    for a in range(1, steps):
        launch(left_copy(a))
        launch(main_copy(a))
    launch(twin_copy(0, 0))
    flags = absorb(0, 0, 0)

    weight_f32[...] = ow_ref[...].astype(jnp.float32)
    for e in range(channels):
        part = weight_f32[pl.ds(e, channels, stride=channels), :]
        outer[e * channels : (e + 1) * channels, 0:pair] = part.astype(jnp.bfloat16)
    weight_t[...] = outer[:, 0:pair].astype(jnp.float32).T.astype(jnp.bfloat16)

    for a in range(1, steps):
        left_copy(steps - a).wait_recv()
        main_copy(steps - a).wait_recv()
        launch(side_copy(a))
        launch(twin_copy(a, 0))
        flags = flags + absorb(a, 0, 0)
    for a in range(steps):
        side_copy(a).wait_recv()
        launch(twin_copy(a, 1))
        flags = flags + absorb(a, 1, 0)
    for b in range(2):
        for a in range(steps):
            twin_copy(a, b).wait_recv()
            flags = flags + absorb(a, b, 1)

    live = jnp.sum(jnp.sum(flags, axis=0, keepdims=True), axis=1, keepdims=True)

    ordered = jnp.concatenate(
        [left_f32[pl.ds(i, count, stride=rows_here), :] for i in range(rows_here)], axis=0
    )
    turned = ordered.T
    left_all = jnp.concatenate(
        [
            jnp.concatenate(
                [
                    turned[s * channels : (s + 1) * channels, i * count : (i + 1) * count]
                    for s in range(seqs)
                ],
                axis=1,
            )
            for i in range(rows_here)
        ],
        axis=0,
    ).astype(jnp.bfloat16)

    for j in range(blocks):
        for e in range(channels):
            base = j * count * block_rows
            piece = jnp.concatenate(
                [
                    right_f32[pl.ds(base + s * channels + e, count, stride=block_rows), :]
                    for s in range(seqs)
                ],
                axis=0,
            ).astype(jnp.bfloat16)
            sums = jnp.dot(left_all, piece, preferred_element_type=jnp.float32)
            sums = sums.astype(jnp.bfloat16)
            for i in range(rows_here):
                outer[e * channels : (e + 1) * channels, i * LANES : (i + 1) * LANES] = sums[
                    i * channels : (i + 1) * channels, :
                ]
        crop_cols = crop_ref[:, j * LANES : (j + 1) * LANES].astype(jnp.float32)
        projected = jnp.dot(weight_t[...], outer[...], preferred_element_type=jnp.float32)
        for i in range(rows_here):
            mask = crop_smem[me * rows_here + i].astype(jnp.float32) * crop_cols
            scale = mask / jnp.maximum(live * mask, 1.0)
            block = projected[:, i * LANES : (i + 1) * LANES] * scale
            out_ref[i, j * LANES : (j + 1) * LANES, :] = (block.T + ob_ref[...]).astype(
                out_ref.dtype
            )

    for one in started:
        one.wait_send()


def per_device(
    alignment,
    seq_flags,
    crop_flags,
    norm_gain,
    norm_bias,
    left_weight,
    left_bias,
    right_weight,
    right_bias,
    out_weight,
    out_bias,
):
    devices = lax.axis_size("row")
    steps = devices // 4
    seqs, residues, _ = alignment.shape
    channels = left_weight.shape[1]
    pair = out_weight.shape[1]
    rows_here = residues // devices
    block_rows = seqs * channels
    total_rows = 4 * rows_here + TILE + block_rows * (residues // LANES)
    vmem = pl.BlockSpec(memory_space=pltpu.VMEM)
    smem = pl.BlockSpec(memory_space=pltpu.SMEM)
    return pl.pallas_call(
        functools.partial(kernel, steps),
        out_shape=jax.ShapeDtypeStruct((rows_here, residues, pair), jnp.bfloat16),
        in_specs=[smem, smem] + [vmem] * 10,
        out_specs=vmem,
        scratch_shapes=[
            pltpu.VMEM((steps, 2, 2, total_rows, LANES), jnp.bfloat16),
            pltpu.VMEM((residues, seqs * channels), jnp.bfloat16),
            pltpu.VMEM((residues // LANES * devices * block_rows, LANES), jnp.float32),
            pltpu.VMEM((devices * rows_here, seqs * channels), jnp.float32),
            pltpu.VMEM((channels * channels, pair), jnp.float32),
            pltpu.VMEM((pair, channels * channels), jnp.bfloat16),
            pltpu.VMEM((channels * channels, rows_here * LANES), jnp.bfloat16),
            pltpu.SemaphoreType.DMA((len(copy_plan(steps)),)),
            pltpu.SemaphoreType.DMA((steps, 2, 2)),
            pltpu.SemaphoreType.DMA((steps,)),
        ],
        compiler_params=pltpu.CompilerParams(
            collective_id=0, has_side_effects=True, vmem_limit_bytes=48 * 1024 * 1024
        ),
    )(
        seq_flags,
        crop_flags,
        alignment,
        crop_flags.reshape(1, residues),
        norm_gain.reshape(1, -1),
        norm_bias.reshape(1, -1),
        left_weight.T,
        left_bias.reshape(1, -1),
        right_weight.T,
        right_bias.reshape(1, -1),
        out_weight,
        out_bias.reshape(1, -1),
    )


def solution(mesh):
    return jax.shard_map(
        per_device,
        mesh=mesh,
        in_specs=(
            P(("grp", "row"), None, None),
            P(("grp", "row")),
            P("grp"),
            P(),
            P(),
            P(),
            P(),
            P(),
            P(),
            P(),
            P(),
        ),
        out_specs=P(("grp", "row"), None, None),
        check_vma=False,
    )
```

```python
import functools

import jax
import jax.numpy as jnp
from jax import lax
from jax.experimental import pallas as pl
from jax.experimental.pallas import tpu as pltpu
from jax.sharding import PartitionSpec as P

LANES = 128
TILE = 16
INPUTS = 12


def copy_plan(steps):
    plan = []
    for a in range(1, steps):
        plan.append(("left", a))
        plan.append(("main", a))
    for a in range(steps):
        plan.append(("side", a))
    for b in range(2):
        for a in range(steps):
            plan.append(("twin", a, b))
    return {name: number for number, name in enumerate(plan)}


def kernel(
    steps,
    *refs,
):
    sources, out_ref, refs = refs[:INPUTS], refs[INPUTS], refs[INPUTS + 1 :]
    inputs, refs = refs[:INPUTS], refs[INPUTS:]
    (
        x_ref,
        gain_ref,
        shift_ref,
        rw_ref,
        rb_ref,
        lw_ref,
        lb_ref,
        flags_ref,
        ow_ref,
        crop_smem,
        crop_ref,
        ob_ref,
    ) = inputs
    (
        held,
        left_src,
        right_f32,
        left_f32,
        weight_f32,
        weight_t,
        outer,
        send_sem,
        recv_sem,
        recv_left,
        load_sem,
    ) = refs
    loads = [
        pltpu.make_async_copy(source, there, load_sem.at[number])
        for number, (source, there) in enumerate(zip(sources, inputs))
    ]
    for load in loads:
        load.start()
    seqs, residues, width = x_ref.shape
    channels = lw_ref.shape[0]
    rows_here = out_ref.shape[0]
    pair = out_ref.shape[2]
    count = steps * 4
    blocks = residues // LANES
    left_rows = 4 * rows_here
    head = left_rows + TILE
    block_rows = seqs * channels
    total_rows = held.shape[3]
    plan = copy_plan(steps)

    me = lax.axis_index("row")
    core = lax.rem(me, 2)
    side = lax.rem(lax.div(me, 2), 2)
    line = lax.div(me, 4)

    def at_line(offset):
        return lax.rem(line + offset, steps) * 4 + side * 2 + core

    twin = me + 1 - 2 * core
    across = me + 2 - 4 * side

    barrier = pltpu.get_barrier_semaphore()
    peers = [at_line(a) for a in range(1, steps)] + [across, twin]
    for peer in peers:
        pl.semaphore_signal(
            barrier, inc=1, device_id={"row": peer}, device_id_type=pl.DeviceIdType.MESH
        )

    def copy(src, dst, name, recv, device):
        return pltpu.make_async_remote_copy(
            src_ref=src,
            dst_ref=dst,
            send_sem=send_sem.at[plan[name]],
            recv_sem=recv,
            device_id={"row": device},
            device_id_type=pl.DeviceIdType.MESH,
        )

    for load in loads[:8]:
        load.wait()
    values = x_ref[...].astype(jnp.float32).reshape(seqs * residues, width)
    average = jnp.mean(values, axis=-1, keepdims=True)
    centred = values - average
    variance = jnp.mean(centred * centred, axis=-1, keepdims=True)
    normed = centred * lax.rsqrt(variance + 1e-05) * gain_ref[...] + shift_ref[...]
    high = normed.astype(jnp.bfloat16)
    low = (normed - high.astype(jnp.float32)).astype(jnp.bfloat16)

    def dot_t(a, b):
        return lax.dot_general(a, b, (((1,), (1,)), ((), ())), preferred_element_type=jnp.float32)

    right = dot_t(rw_ref[...], high) + dot_t(rw_ref[...], low)
    row_of = lax.broadcasted_iota(jnp.int32, (channels, channels), 0)
    col_of = lax.broadcasted_iota(jnp.int32, (channels, channels), 1)
    right_bias = jnp.sum(jnp.where(row_of == col_of, rb_ref[...], 0.0), axis=1, keepdims=True)
    right = right + right_bias
    lane_of = lax.broadcasted_iota(jnp.int32, (TILE, LANES), 1)
    row_id = lax.broadcasted_iota(jnp.int32, (TILE, LANES), 0)
    flag_tile = jnp.zeros((TILE, LANES), jnp.float32)
    for s in range(seqs):
        flag = flags_ref[s].astype(jnp.float32)
        flag_tile = jnp.where((lane_of == s % LANES) & (row_id == s // LANES), flag, flag_tile)
        for b in range(blocks):
            start = s * residues + b * LANES
            piece = (right[:, start : start + LANES] * flag).astype(jnp.bfloat16)
            place = head + b * block_rows + s * channels
            held[0, 0, 0, place : place + channels, :] = piece
    held[0, 0, 0, left_rows:head, :] = flag_tile.astype(jnp.bfloat16)

    left = dot_t(high, lw_ref[...]) + dot_t(low, lw_ref[...]) + lb_ref[...]
    left = jnp.concatenate(
        [left[s * residues : (s + 1) * residues, :] for s in range(seqs)], axis=1
    )
    left_src[...] = left.astype(jnp.bfloat16)
    own = pl.multiple_of(line * left_rows, left_rows)
    held[0, 0, 0, 0:left_rows, :] = left_src[pl.ds(own, left_rows), :]

    pl.semaphore_wait(barrier, len(peers))

    main = pl.ds(left_rows, total_rows - left_rows)
    upper = pl.ds(0, left_rows)
    started = []

    def left_copy(a):
        there = lax.rem(line + a, steps)
        rows = pl.ds(pl.multiple_of(there * left_rows, left_rows), left_rows)
        slot = (steps - a) % steps
        return copy(
            left_src.at[rows, :],
            held.at[slot, 0, 0, upper, :],
            ("left", a),
            recv_left.at[slot],
            at_line(a),
        )

    def main_copy(a):
        slot = (steps - a) % steps
        return copy(
            held.at[0, 0, 0, main, :],
            held.at[slot, 0, 0, main, :],
            ("main", a),
            recv_sem.at[slot, 0, 0],
            at_line(a),
        )

    def side_copy(a):
        return copy(
            held.at[a, 0, 0], held.at[a, 1, 0], ("side", a), recv_sem.at[a, 1, 0], across
        )

    def twin_copy(a, b):
        return copy(
            held.at[a, b, 0], held.at[a, b, 1], ("twin", a, b), recv_sem.at[a, b, 1], twin
        )

    def launch(one):
        one.start()
        started.append(one)

    def absorb(a, b, c):
        k = (c * 2 + b) * steps + a
        for j in range(blocks):
            rows = held[a, b, c, head + j * block_rows : head + (j + 1) * block_rows, :]
            base = (j * count + k) * block_rows
            right_f32[base : base + block_rows, :] = rows.astype(jnp.float32)
        start = pl.multiple_of(side * 2 * rows_here, 2 * rows_here)
        mine = held[a, b, c, pl.ds(start, 2 * rows_here), :].astype(jnp.float32)
        mine = jnp.where(core == 0, mine[:rows_here, :], mine[rows_here:, :])
        left_f32[k * rows_here : (k + 1) * rows_here, :] = mine
        return held[a, b, c, left_rows:head, :].astype(jnp.float32)

    launch(side_copy(0))
    for a in range(1, steps):
        launch(left_copy(a))
        launch(main_copy(a))
    launch(twin_copy(0, 0))
    flags = absorb(0, 0, 0)

    for load in loads[8:]:
        load.wait()
    weight_f32[...] = ow_ref[...].astype(jnp.float32)
    for e in range(channels):
        part = weight_f32[pl.ds(e, channels, stride=channels), :]
        outer[e * channels : (e + 1) * channels, 0:pair] = part.astype(jnp.bfloat16)
    weight_t[...] = outer[:, 0:pair].astype(jnp.float32).T.astype(jnp.bfloat16)

    for a in range(1, steps):
        left_copy(steps - a).wait_recv()
        main_copy(steps - a).wait_recv()
        launch(side_copy(a))
        launch(twin_copy(a, 0))
        flags = flags + absorb(a, 0, 0)
    for a in range(steps):
        side_copy(a).wait_recv()
        launch(twin_copy(a, 1))
        flags = flags + absorb(a, 1, 0)
    for b in range(2):
        for a in range(steps):
            twin_copy(a, b).wait_recv()
            flags = flags + absorb(a, b, 1)

    live = jnp.sum(jnp.sum(flags, axis=0, keepdims=True), axis=1, keepdims=True)

    ordered = jnp.concatenate(
        [left_f32[pl.ds(i, count, stride=rows_here), :] for i in range(rows_here)], axis=0
    )
    turned = ordered.T
    left_all = jnp.concatenate(
        [
            jnp.concatenate(
                [
                    turned[s * channels : (s + 1) * channels, i * count : (i + 1) * count]
                    for s in range(seqs)
                ],
                axis=1,
            )
            for i in range(rows_here)
        ],
        axis=0,
    ).astype(jnp.bfloat16)

    for j in range(blocks):
        for e in range(channels):
            base = j * count * block_rows
            piece = jnp.concatenate(
                [
                    right_f32[pl.ds(base + s * channels + e, count, stride=block_rows), :]
                    for s in range(seqs)
                ],
                axis=0,
            ).astype(jnp.bfloat16)
            sums = jnp.dot(left_all, piece, preferred_element_type=jnp.float32)
            sums = sums.astype(jnp.bfloat16)
            for i in range(rows_here):
                outer[e * channels : (e + 1) * channels, i * LANES : (i + 1) * LANES] = sums[
                    i * channels : (i + 1) * channels, :
                ]
        crop_cols = crop_ref[:, j * LANES : (j + 1) * LANES].astype(jnp.float32)
        projected = jnp.dot(weight_t[...], outer[...], preferred_element_type=jnp.float32)
        for i in range(rows_here):
            mask = crop_smem[me * rows_here + i].astype(jnp.float32) * crop_cols
            scale = mask / jnp.maximum(live * mask, 1.0)
            block = projected[:, i * LANES : (i + 1) * LANES] * scale
            out_ref[i, j * LANES : (j + 1) * LANES, :] = (block.T + ob_ref[...]).astype(
                out_ref.dtype
            )

    for one in started:
        one.wait_send()


def per_device(
    alignment,
    seq_flags,
    crop_flags,
    norm_gain,
    norm_bias,
    left_weight,
    left_bias,
    right_weight,
    right_bias,
    out_weight,
    out_bias,
):
    devices = lax.axis_size("row")
    steps = devices // 4
    seqs, residues, _ = alignment.shape
    channels = left_weight.shape[1]
    pair = out_weight.shape[1]
    rows_here = residues // devices
    block_rows = seqs * channels
    total_rows = 4 * rows_here + TILE + block_rows * (residues // LANES)
    operands = [
        alignment,
        norm_gain.reshape(1, -1),
        norm_bias.reshape(1, -1),
        right_weight.T,
        right_bias.reshape(1, -1),
        left_weight.T,
        left_bias.reshape(1, -1),
        seq_flags,
        out_weight,
        crop_flags,
        crop_flags.reshape(1, residues),
        out_bias.reshape(1, -1),
    ]
    spaces = [pltpu.VMEM] * INPUTS
    spaces[7] = spaces[9] = pltpu.SMEM
    return pl.pallas_call(
        functools.partial(kernel, steps),
        out_shape=jax.ShapeDtypeStruct((rows_here, residues, pair), jnp.bfloat16),
        in_specs=[pl.BlockSpec(memory_space=pltpu.HBM)] * INPUTS,
        out_specs=pl.BlockSpec(memory_space=pltpu.VMEM),
        scratch_shapes=[space(one.shape, one.dtype) for space, one in zip(spaces, operands)]
        + [
            pltpu.VMEM((steps, 2, 2, total_rows, LANES), jnp.bfloat16),
            pltpu.VMEM((residues, seqs * channels), jnp.bfloat16),
            pltpu.VMEM((residues // LANES * devices * block_rows, LANES), jnp.float32),
            pltpu.VMEM((devices * rows_here, seqs * channels), jnp.float32),
            pltpu.VMEM((channels * channels, pair), jnp.float32),
            pltpu.VMEM((pair, channels * channels), jnp.bfloat16),
            pltpu.VMEM((channels * channels, rows_here * LANES), jnp.bfloat16),
            pltpu.SemaphoreType.DMA((len(copy_plan(steps)),)),
            pltpu.SemaphoreType.DMA((steps, 2, 2)),
            pltpu.SemaphoreType.DMA((steps,)),
            pltpu.SemaphoreType.DMA((INPUTS,)),
        ],
        compiler_params=pltpu.CompilerParams(
            collective_id=0, has_side_effects=True, vmem_limit_bytes=60 * 1024 * 1024
        ),
    )(*operands)


def solution(mesh):
    return jax.shard_map(
        per_device,
        mesh=mesh,
        in_specs=(
            P(("grp", "row"), None, None),
            P(("grp", "row")),
            P("grp"),
            P(),
            P(),
            P(),
            P(),
            P(),
            P(),
            P(),
            P(),
        ),
        out_specs=P(("grp", "row"), None, None),
        check_vma=False,
    )
```

```python
import functools

import jax
import jax.numpy as jnp
from jax import lax
from jax.experimental import pallas as pl
from jax.experimental.pallas import tpu as pltpu
from jax.sharding import PartitionSpec as P

LANES = 128
TILE = 16
INPUTS = 12


def copy_plan(steps):
    plan = []
    for a in range(1, steps):
        plan.append(("left", a))
        plan.append(("main", a))
    for a in range(steps):
        plan.append(("side", a))
    for b in range(2):
        for a in range(steps):
            plan.append(("twin", a, b))
    return {name: number for number, name in enumerate(plan)}


def kernel(
    steps,
    *refs,
):
    sources, out_ref, refs = refs[:INPUTS], refs[INPUTS], refs[INPUTS + 1 :]
    inputs, refs = refs[:INPUTS], refs[INPUTS:]
    (
        x_ref,
        gain_ref,
        shift_ref,
        rw_ref,
        rb_ref,
        lw_ref,
        lb_ref,
        flags_ref,
        ow_ref,
        crop_smem,
        crop_ref,
        ob_ref,
    ) = inputs
    (
        held,
        left_src,
        right_f32,
        left_f32,
        weight_f32,
        weight_t,
        outer,
        send_sem,
        recv_sem,
        recv_left,
        load_sem,
    ) = refs
    loads = [
        pltpu.make_async_copy(source, there, load_sem.at[number])
        for number, (source, there) in enumerate(zip(sources, inputs))
    ]
    for load in loads:
        load.start()
    seqs, residues, width = x_ref.shape
    channels = lw_ref.shape[0]
    rows_here = out_ref.shape[0]
    pair = out_ref.shape[2]
    count = steps * 4
    blocks = residues // LANES
    left_rows = 4 * rows_here
    near = (steps - 1) * left_rows
    flag_row = steps * left_rows
    head = flag_row + TILE
    block_rows = seqs * channels
    total_rows = held.shape[3]
    plan = copy_plan(steps)

    me = lax.axis_index("row")
    core = lax.rem(me, 2)
    side = lax.rem(lax.div(me, 2), 2)
    line = lax.div(me, 4)

    def other(bits):
        there = line
        bit = 1
        while bit <= bits:
            if bits & bit:
                there = there + bit - 2 * bit * lax.rem(lax.div(there, bit), 2)
            bit *= 2
        return there

    def at_line(bits):
        return other(bits) * 4 + side * 2 + core

    twin = me + 1 - 2 * core
    across = me + 2 - 4 * side

    barrier = pltpu.get_barrier_semaphore()
    hops = [1 << t for t in range(steps.bit_length() - 1)]
    peers = [at_line(bit) for bit in hops] + [across, twin]
    for peer in peers:
        pl.semaphore_signal(
            barrier, inc=1, device_id={"row": peer}, device_id_type=pl.DeviceIdType.MESH
        )

    def copy(src, dst, name, recv, device):
        return pltpu.make_async_remote_copy(
            src_ref=src,
            dst_ref=dst,
            send_sem=send_sem.at[plan[name]],
            recv_sem=recv,
            device_id={"row": device},
            device_id_type=pl.DeviceIdType.MESH,
        )

    for load in loads[:8]:
        load.wait()
    values = x_ref[...].astype(jnp.float32).reshape(seqs * residues, width)
    average = jnp.mean(values, axis=-1, keepdims=True)
    centred = values - average
    variance = jnp.mean(centred * centred, axis=-1, keepdims=True)
    normed = centred * lax.rsqrt(variance + 1e-05) * gain_ref[...] + shift_ref[...]
    high = normed.astype(jnp.bfloat16)
    low = (normed - high.astype(jnp.float32)).astype(jnp.bfloat16)

    def dot_t(a, b):
        return lax.dot_general(a, b, (((1,), (1,)), ((), ())), preferred_element_type=jnp.float32)

    right = dot_t(rw_ref[...], high) + dot_t(rw_ref[...], low)
    row_of = lax.broadcasted_iota(jnp.int32, (channels, channels), 0)
    col_of = lax.broadcasted_iota(jnp.int32, (channels, channels), 1)
    right_bias = jnp.sum(jnp.where(row_of == col_of, rb_ref[...], 0.0), axis=1, keepdims=True)
    right = right + right_bias
    lane_of = lax.broadcasted_iota(jnp.int32, (TILE, LANES), 1)
    row_id = lax.broadcasted_iota(jnp.int32, (TILE, LANES), 0)
    flag_tile = jnp.zeros((TILE, LANES), jnp.float32)
    for s in range(seqs):
        flag = flags_ref[s].astype(jnp.float32)
        flag_tile = jnp.where((lane_of == s % LANES) & (row_id == s // LANES), flag, flag_tile)
        for b in range(blocks):
            start = s * residues + b * LANES
            piece = (right[:, start : start + LANES] * flag).astype(jnp.bfloat16)
            place = head + b * block_rows + s * channels
            held[0, 0, 0, place : place + channels, :] = piece
    held[0, 0, 0, flag_row:head, :] = flag_tile.astype(jnp.bfloat16)

    left = dot_t(high, lw_ref[...]) + dot_t(low, lw_ref[...]) + lb_ref[...]
    left = jnp.concatenate(
        [left[s * residues : (s + 1) * residues, :] for s in range(seqs)], axis=1
    )
    left_src[...] = left.astype(jnp.bfloat16)
    for q in range(steps):
        start = pl.multiple_of(other(q) * left_rows, left_rows)
        place = (steps - 1 - q) * left_rows
        held[0, 0, 0, place : place + left_rows, :] = left_src[pl.ds(start, left_rows), :]

    pl.semaphore_wait(barrier, len(peers))

    main = pl.ds(flag_row, total_rows - flag_row)
    tail = pl.ds(near, total_rows - near)
    started = []

    def left_copy(a):
        bit = a & -a
        return copy(
            held.at[a - bit, 0, 0, pl.ds((steps - 2 * bit) * left_rows, bit * left_rows), :],
            held.at[a, 0, 0, pl.ds((steps - bit) * left_rows, bit * left_rows), :],
            ("left", a),
            recv_left.at[a],
            at_line(bit),
        )

    def main_copy(a):
        bit = a & -a
        return copy(
            held.at[a - bit, 0, 0, main, :],
            held.at[a, 0, 0, main, :],
            ("main", a),
            recv_sem.at[a, 0, 0],
            at_line(bit),
        )

    def side_copy(a):
        return copy(
            held.at[a, 0, 0, tail, :],
            held.at[a, 1, 0, tail, :],
            ("side", a),
            recv_sem.at[a, 1, 0],
            across,
        )

    def twin_copy(a, b):
        return copy(
            held.at[a, b, 0, tail, :],
            held.at[a, b, 1, tail, :],
            ("twin", a, b),
            recv_sem.at[a, b, 1],
            twin,
        )

    def launch(one):
        one.start()
        started.append(one)

    def absorb(a, b, c):
        k = (c * 2 + b) * steps + a
        for j in range(blocks):
            rows = held[a, b, c, head + j * block_rows : head + (j + 1) * block_rows, :]
            base = (j * count + k) * block_rows
            right_f32[base : base + block_rows, :] = rows.astype(jnp.float32)
        start = pl.multiple_of(near + side * 2 * rows_here, 2 * rows_here)
        mine = held[a, b, c, pl.ds(start, 2 * rows_here), :].astype(jnp.float32)
        mine = jnp.where(core == 0, mine[:rows_here, :], mine[rows_here:, :])
        left_f32[k * rows_here : (k + 1) * rows_here, :] = mine
        return held[a, b, c, flag_row:head, :].astype(jnp.float32)

    def spread(a):
        low = a & -a if a else steps
        for bit in reversed(hops):
            if bit < low:
                launch(main_copy(a + bit))
                launch(left_copy(a + bit))
        launch(side_copy(a))
        launch(twin_copy(a, 0))

    spread(0)
    flags = absorb(0, 0, 0)

    for load in loads[8:]:
        load.wait()
    weight_f32[...] = ow_ref[...].astype(jnp.float32)
    for e in range(channels):
        part = weight_f32[pl.ds(e, channels, stride=channels), :]
        outer[e * channels : (e + 1) * channels, 0:pair] = part.astype(jnp.bfloat16)
    weight_t[...] = outer[:, 0:pair].astype(jnp.float32).T.astype(jnp.bfloat16)

    for a in range(1, steps):
        main_copy(a).wait_recv()
        left_copy(a).wait_recv()
        spread(a)
        flags = flags + absorb(a, 0, 0)
    for a in range(steps):
        side_copy(a).wait_recv()
        launch(twin_copy(a, 1))
        flags = flags + absorb(a, 1, 0)
    for b in range(2):
        for a in range(steps):
            twin_copy(a, b).wait_recv()
            flags = flags + absorb(a, b, 1)

    live = jnp.sum(jnp.sum(flags, axis=0, keepdims=True), axis=1, keepdims=True)

    ordered = jnp.concatenate(
        [left_f32[pl.ds(i, count, stride=rows_here), :] for i in range(rows_here)], axis=0
    )
    turned = ordered.T
    left_all = jnp.concatenate(
        [
            jnp.concatenate(
                [
                    turned[s * channels : (s + 1) * channels, i * count : (i + 1) * count]
                    for s in range(seqs)
                ],
                axis=1,
            )
            for i in range(rows_here)
        ],
        axis=0,
    ).astype(jnp.bfloat16)

    for j in range(blocks):
        for e in range(channels):
            base = j * count * block_rows
            piece = jnp.concatenate(
                [
                    right_f32[pl.ds(base + s * channels + e, count, stride=block_rows), :]
                    for s in range(seqs)
                ],
                axis=0,
            ).astype(jnp.bfloat16)
            sums = jnp.dot(left_all, piece, preferred_element_type=jnp.float32)
            sums = sums.astype(jnp.bfloat16)
            for i in range(rows_here):
                outer[e * channels : (e + 1) * channels, i * LANES : (i + 1) * LANES] = sums[
                    i * channels : (i + 1) * channels, :
                ]
        crop_cols = crop_ref[:, j * LANES : (j + 1) * LANES].astype(jnp.float32)
        projected = jnp.dot(weight_t[...], outer[...], preferred_element_type=jnp.float32)
        for i in range(rows_here):
            mask = crop_smem[me * rows_here + i].astype(jnp.float32) * crop_cols
            scale = mask / jnp.maximum(live * mask, 1.0)
            block = projected[:, i * LANES : (i + 1) * LANES] * scale
            out_ref[i, j * LANES : (j + 1) * LANES, :] = (block.T + ob_ref[...]).astype(
                out_ref.dtype
            )

    for one in started:
        one.wait_send()


def per_device(
    alignment,
    seq_flags,
    crop_flags,
    norm_gain,
    norm_bias,
    left_weight,
    left_bias,
    right_weight,
    right_bias,
    out_weight,
    out_bias,
):
    devices = lax.axis_size("row")
    steps = devices // 4
    seqs, residues, _ = alignment.shape
    channels = left_weight.shape[1]
    pair = out_weight.shape[1]
    rows_here = residues // devices
    block_rows = seqs * channels
    total_rows = residues + TILE + block_rows * (residues // LANES)
    operands = [
        alignment,
        norm_gain.reshape(1, -1),
        norm_bias.reshape(1, -1),
        right_weight.T,
        right_bias.reshape(1, -1),
        left_weight.T,
        left_bias.reshape(1, -1),
        seq_flags,
        out_weight,
        crop_flags,
        crop_flags.reshape(1, residues),
        out_bias.reshape(1, -1),
    ]
    spaces = [pltpu.VMEM] * INPUTS
    spaces[7] = spaces[9] = pltpu.SMEM
    return pl.pallas_call(
        functools.partial(kernel, steps),
        out_shape=jax.ShapeDtypeStruct((rows_here, residues, pair), jnp.bfloat16),
        in_specs=[pl.BlockSpec(memory_space=pltpu.HBM)] * INPUTS,
        out_specs=pl.BlockSpec(memory_space=pltpu.VMEM),
        scratch_shapes=[space(one.shape, one.dtype) for space, one in zip(spaces, operands)]
        + [
            pltpu.VMEM((steps, 2, 2, total_rows, LANES), jnp.bfloat16),
            pltpu.VMEM((residues, seqs * channels), jnp.bfloat16),
            pltpu.VMEM((residues // LANES * devices * block_rows, LANES), jnp.float32),
            pltpu.VMEM((devices * rows_here, seqs * channels), jnp.float32),
            pltpu.VMEM((channels * channels, pair), jnp.float32),
            pltpu.VMEM((pair, channels * channels), jnp.bfloat16),
            pltpu.VMEM((channels * channels, rows_here * LANES), jnp.bfloat16),
            pltpu.SemaphoreType.DMA((len(copy_plan(steps)),)),
            pltpu.SemaphoreType.DMA((steps, 2, 2)),
            pltpu.SemaphoreType.DMA((steps,)),
            pltpu.SemaphoreType.DMA((INPUTS,)),
        ],
        compiler_params=pltpu.CompilerParams(
            collective_id=0, has_side_effects=True, vmem_limit_bytes=60 * 1024 * 1024
        ),
    )(*operands)


def solution(mesh):
    return jax.shard_map(
        per_device,
        mesh=mesh,
        in_specs=(
            P(("grp", "row"), None, None),
            P(("grp", "row")),
            P("grp"),
            P(),
            P(),
            P(),
            P(),
            P(),
            P(),
            P(),
            P(),
        ),
        out_specs=P(("grp", "row"), None, None),
        check_vma=False,
    )
```
